32 devices in a mesh: slab: 4 (over z), curve: 8 (over y, x, core).
Axes of the slice: x: 2, y: 2, z: 4, core: 2. Of those that a mesh axis runs over, the one named last changes fastest.
Arguments:
- tracer_state: float32 [6, 125, 8192], P(None, None, ('slab', 'curve')), may hold values from -6 to 6
- inv_size: float32 [8192], P(('slab', 'curve')), may hold values from 1 to 6
- velocity: float32 [3, 6], replicated, may hold values from -1.5 to 1.5
- element_count: int32 [32], P(('slab', 'curve')), may hold values from 128 to 256, as said below
- face_kind: int32 [6, 8192], P(None, ('slab', 'curve')), may hold values from 0 to 5, as said below
- face_owner: int32 [6, 8192], P(None, ('slab', 'curve')), may hold values from 0 to 31, as said below
- face_index: int32 [6, 8192], P(None, ('slab', 'curve')), may hold values from 0 to 1535, as said below
- face_orient: int32 [6, 8192], P(None, ('slab', 'curve')), may hold values from 0 to 3
- hang_owner: int32 [4, 2048], P(None, ('slab', 'curve')), may hold values from 0 to 31, as said below
- hang_index: int32 [4, 2048], P(None, ('slab', 'curve')), may hold values from 0 to 1535, as said below
- hang_orient: int32 [4, 2048], P(None, ('slab', 'curve')), may hold values from 0 to 3
- mirror: int32 [32, 1024], P(('slab', 'curve')), may hold values from -1 to 1535, as said below
Outputs:
- new_state: float32 [6, 125, 8192], P(None, None, ('slab', 'curve'))
- increment: float32 [6, 125, 8192], P(None, None, ('slab', 'curve'))
The draws below stay inside these ranges and needn't reach their ends.
Inputs may be any that keep to these rules, and one draw needn't show every extreme that they name: `element_count`: some device holds 256 live elements. `face_kind`: each device has exactly 64 sides of kind 5, whose face_index values are 0 to 63, each once. `face_owner`: A side of kind 5 has its own device as owner; every owner lies within 4 ranks of the device. `face_index`: for a remote owner the index is a slot below 128 that is filled in mirror; every filled slot to a device is named by exactly one side or hanging entry of that device. Local indices name faces of live elements. `hang_owner`: every owner lies within 4 ranks of the device. `hang_index`: same convention as face_index. `mirror`: filled entries name faces of live elements of the sender; columns whose destination lies outside the ranks are empty; some device receives all 128 slots filled from each of its 8 neighbours.
All inputs are finite; a program needn't handle non-finite values.
Results may differ from the reference program's by a relative error of at most 0.0003.
Values sent between devices are 32-bit elements; how exact they have to be, the bound alone decides.
A program may use at most 128 MiB of HBM per device.

```python
import math
import jax
import jax.numpy as jnp
import numpy as np
from jax import lax

TRACERS = 6
E_DEV = 256
NEAR = 4
SLOTS = 128
HANG_DEV = 64
ELEMS = 8192
N_SLAB = 4
N_CURVE = 8


def forest(key):
    devices_all = N_SLAB * N_CURVE
    faces_total = 6 * E_DEV
    entries = faces_total + 4 * HANG_DEV
    columns = 2 * NEAR
    keys = jax.random.split(key, 7)
    shortfall = jax.random.randint(keys[0], (devices_all,), 0, E_DEV // 2 + 1)
    fullest = jax.random.randint(keys[1], (), 0, devices_all)
    rank_ids = jnp.arange(devices_all, dtype=jnp.int32)
    counts = jnp.where(rank_ids == fullest, E_DEV, E_DEV - shortfall).astype(jnp.int32)
    offsets = jnp.concatenate([jnp.arange(-NEAR, 0, dtype=jnp.int32), jnp.arange(1, NEAR + 1, dtype=jnp.int32)])
    busiest = jax.random.randint(keys[2], (), NEAR, devices_all - NEAR)
    targets = rank_ids[:, None] + offsets[None, :]
    valid = (targets >= 0) & (targets < devices_all)
    filled = jax.random.randint(keys[3], (devices_all, columns, SLOTS), 0, 5) < 3
    filled = filled | (targets == busiest)[:, :, None]
    filled = filled & valid[:, :, None]
    sent_elem = jax.random.randint(keys[4], (devices_all, columns, SLOTS), 0, counts[:, None, None])
    sent_side = jax.random.randint(keys[5], (devices_all, columns, SLOTS), 0, 6)
    mirror = jnp.where(filled, sent_side * E_DEV + sent_elem, -1).astype(jnp.int32).reshape(devices_all, columns * SLOTS)

    def one_device(rank_now, key_now):
        part_keys = jax.random.split(key_now, 7)
        senders = rank_now - offsets
        sender_ok = (senders >= 0) & (senders < devices_all)
        safe_senders = jnp.clip(senders, 0, devices_all - 1)
        incoming = filled[safe_senders, jnp.arange(columns, dtype=jnp.int32)] & sender_ok[:, None]
        incoming = incoming.reshape(-1)
        received = jnp.sum(incoming.astype(jnp.int32))
        slot_order = jnp.argsort(jnp.where(incoming, 0, 1).astype(jnp.int32), stable=True).astype(jnp.int32)
        face_perm = jax.random.permutation(part_keys[0], faces_total).astype(jnp.int32)
        coarse = face_perm < HANG_DEV
        roll_die = jax.random.randint(part_keys[1], (faces_total,), 0, 10)
        fine_child = jax.random.randint(part_keys[2], (faces_total,), 1, 5)
        kinds = jnp.where(coarse, 5, jnp.where(roll_die < 6, 0, fine_child)).astype(jnp.int32)
        excluded = jnp.concatenate([coarse, jnp.zeros((4 * HANG_DEV,), dtype=bool)]).astype(jnp.int32)
        priority = jax.random.permutation(part_keys[3], entries).astype(jnp.int32) + entries * excluded
        entry_rank = jnp.argsort(jnp.argsort(priority, stable=True), stable=True).astype(jnp.int32)
        remote = entry_rank < received
        slot_id = slot_order[jnp.minimum(entry_rank, columns * SLOTS - 1)]
        local_elem = jax.random.randint(part_keys[4], (entries,), 0, counts[rank_now])
        local_side = jax.random.randint(part_keys[5], (entries,), 0, 6)
        owners = jnp.where(remote, safe_senders[slot_id // SLOTS], rank_now).astype(jnp.int32)
        indices = jnp.where(remote, slot_id % SLOTS, local_side * E_DEV + local_elem).astype(jnp.int32)
        indices = jnp.concatenate([jnp.where(coarse, face_perm, indices[:faces_total]), indices[faces_total:]])
        turns = jax.random.randint(part_keys[6], (entries,), 0, 4).astype(jnp.int32)
        return (kinds, owners, indices, turns)
    kinds, owners, indices, turns = jax.vmap(one_device)(rank_ids, jax.random.split(keys[6], devices_all))

    def spread_faces(array):
        return jnp.transpose(array[:, :faces_total].reshape(devices_all, 6, E_DEV), (1, 0, 2)).reshape(6, devices_all * E_DEV)

    def spread_hang(array):
        return jnp.transpose(array[:, faces_total:].reshape(devices_all, 4, HANG_DEV), (1, 0, 2)).reshape(4, devices_all * HANG_DEV)
    face_kinds = jnp.transpose(kinds.reshape(devices_all, 6, E_DEV), (1, 0, 2)).reshape(6, devices_all * E_DEV)
    return (counts, face_kinds, spread_faces(owners), spread_faces(indices), spread_faces(turns), spread_hang(owners), spread_hang(indices), spread_hang(turns), mirror)


def draw_element_count(key, part):
    return forest(key)[0]


def draw_face_kind(key, part):
    return forest(key)[1]


def draw_face_owner(key, part):
    return forest(key)[2]


def draw_face_index(key, part):
    return forest(key)[3]


def draw_face_orient(key, part):
    return forest(key)[4]


def draw_hang_owner(key, part):
    return forest(key)[5]


def draw_hang_index(key, part):
    return forest(key)[6]


def draw_hang_orient(key, part):
    return forest(key)[7]


def draw_mirror(key, part):
    return forest(key)[8]


def draw_inv_size(key, part):
    key = jax.random.fold_in(key, 17)
    devices_all = N_SLAB * N_CURVE
    total_cols = E_DEV * devices_all
    position = (jnp.arange(total_cols, dtype=jnp.int32) // E_DEV).astype(jnp.float32)
    grading = 3.0 ** (position / max(devices_all - 1, 1))
    factor = jnp.exp(jax.random.uniform(key, (total_cols,), jnp.float32, 0.0, math.log(2.0)))
    return (grading * factor).astype(jnp.float32)


def level_of(rng, dims, shards, least, high):
    def one(axis_at, shards_of):
        draws = jax.random.uniform(jax.random.fold_in(jax.random.fold_in(rng, 6), axis_at), (shards_of,), jnp.float32, least / len(shards), high / len(shards))
        return jnp.repeat(jnp.exp(draws), dims[axis_at] // shards_of).reshape((-1,) + (1,) * (len(dims) - axis_at - 1))

    loudness = one(*shards[0])
    for cut in shards[1:]:
        loudness = loudness * one(*cut)
    return loudness


def normal_values(rng, shape, scale, reach, cuts=(), kind=jnp.bfloat16):
    drawn = jax.random.normal(rng, shape, jnp.float32) * scale
    if len(cuts) > 0:
        drawn = level_of(rng, shape, cuts, -0.22, 0.18) * drawn
    return jnp.clip(drawn, min=-reach, max=reach).astype(kind)


def setup_inputs(seed: int = 0) -> dict:
    key_of = jax.random.split(jax.random.key(seed), 13)
    return {
        "tracer_state": normal_values(key_of[0], (TRACERS, 125, ELEMS), 1.0, 6.0, ((2, 32),), jnp.float32),
        "inv_size": draw_inv_size(jax.random.fold_in(key_of[12], 71), 0),
        "velocity": jnp.clip(jax.random.uniform(key_of[2], (3, TRACERS), jnp.float32, -1.5, 1.5), -1.5, 1.5),
        "element_count": draw_element_count(jax.random.fold_in(key_of[12], 71), 0),
        "face_kind": draw_face_kind(jax.random.fold_in(key_of[12], 71), 0),
        "face_owner": draw_face_owner(jax.random.fold_in(key_of[12], 71), 0),
        "face_index": draw_face_index(jax.random.fold_in(key_of[12], 71), 0),
        "face_orient": draw_face_orient(jax.random.fold_in(key_of[12], 71), 0),
        "hang_owner": draw_hang_owner(jax.random.fold_in(key_of[12], 71), 0),
        "hang_index": draw_hang_index(jax.random.fold_in(key_of[12], 71), 0),
        "hang_orient": draw_hang_orient(jax.random.fold_in(key_of[12], 71), 0),
        "mirror": draw_mirror(jax.random.fold_in(key_of[12], 71), 0),
    }


B_ONE = 1432997174477.0 / 9575080441755.0
A_TWO = -567301805773.0 / 1357537059087.0
B_TWO = 5161836677717.0 / 13612068292357.0
COURANT = 0.3

def node_tables():
    points = np.array([-1.0, -math.sqrt(3.0 / 7.0), 0.0, math.sqrt(3.0 / 7.0), 1.0])
    weights = np.array([0.1, 49.0 / 90.0, 32.0 / 45.0, 49.0 / 90.0, 0.1])
    return (points, weights)

def lagrange_at(points, targets):
    values = np.ones((len(targets), len(points)))
    for column in range(len(points)):
        for another in range(len(points)):
            if another != column:
                values[:, column] *= (targets - points[another]) / (points[column] - points[another])
    return values

def derivative_table(points):
    count_pts = len(points)
    scaled = np.array([np.prod([points[column] - points[another] for another in range(count_pts) if another != column]) for column in range(count_pts)])
    result = np.zeros((count_pts, count_pts))
    for row_at in range(count_pts):
        for column in range(count_pts):
            if row_at != column:
                result[row_at, column] = scaled[row_at] / scaled[column] / (points[row_at] - points[column])
        result[row_at, row_at] = sum((1.0 / (points[row_at] - points[another]) for another in range(count_pts) if another != row_at))
    return result

def all_tables(dtype_now):
    points, weights = node_tables()
    lower_half = lagrange_at(points, (points - 1.0) / 2.0)
    upper_half = lagrange_at(points, (points + 1.0) / 2.0)
    proj_lower = 0.5 * (lower_half.T * weights[None, :]) / weights[:, None]
    proj_upper = 0.5 * (upper_half.T * weights[None, :]) / weights[:, None]
    interp = jnp.asarray(np.stack([lower_half, upper_half]), dtype=dtype_now)
    project = jnp.asarray(np.stack([proj_lower, proj_upper]), dtype=dtype_now)
    slopes = jnp.asarray(derivative_table(points), dtype=dtype_now)
    return (interp, project, slopes)

def face_traces(volume):
    return jnp.stack([volume[:, 0], volume[:, -1], volume[:, :, 0], volume[:, :, -1], volume[:, :, :, 0], volume[:, :, :, -1]], axis=3)

def orient_faces(traces, turn_bits):
    partway = jnp.where(turn_bits % 2 == 1, jnp.flip(traces, 1), traces)
    return jnp.where(turn_bits // 2 == 1, jnp.flip(partway, 2), partway)

def child_map(traces, child_pos, matrices):
    high = lax.Precision.HIGHEST
    low_first = jnp.einsum('ai,tijf->tajf', matrices[0], traces, precision=high)
    high_first = jnp.einsum('ai,tijf->tajf', matrices[1], traces, precision=high)
    partway = jnp.where(child_pos % 2 == 1, high_first, low_first)
    low_second = jnp.einsum('bj,tajf->tabf', matrices[0], partway, precision=high)
    high_second = jnp.einsum('bj,tajf->tabf', matrices[1], partway, precision=high)
    return jnp.where(child_pos // 2 == 1, high_second, low_second)

def exterior_traces(sources, tracers, face_source, kinds, face_turns, hang_source, hang_turns, coarse_pick, interp, project):
    faces_total = face_source.shape[0]
    fetched = jnp.take(sources, face_source, axis=1).reshape(tracers, 5, 5, faces_total)
    fetched = orient_faces(fetched, face_turns)
    refined = child_map(fetched, jnp.clip(kinds - 1, 0, 3), interp)
    hang_count = hang_source.shape[0] // 4
    children = jnp.take(sources, hang_source, axis=1).reshape(tracers, 5, 5, 4 * hang_count)
    children = orient_faces(children, hang_turns)
    child_ids = jnp.arange(4 * hang_count, dtype=jnp.int32) // hang_count
    projected = child_map(children, child_ids, project).reshape(tracers, 5, 5, 4, hang_count)
    projected = projected[:, :, :, 0] + projected[:, :, :, 1] + projected[:, :, :, 2] + projected[:, :, :, 3]
    coarse = jnp.take(projected, coarse_pick, axis=3)
    result = jnp.where(kinds == 0, fetched, refined)
    return jnp.where(kinds == 5, coarse, result)

def tendency(state_now, inv_size, outside, velocity, slopes):
    high = lax.Precision.HIGHEST
    tracers = state_now.shape[0]
    elements = state_now.shape[2]
    volume = state_now.reshape(tracers, 5, 5, 5, elements)
    along_x = jnp.einsum('ai,tijke->tajke', slopes, volume, precision=high)
    along_y = jnp.einsum('bj,tijke->tibke', slopes, volume, precision=high)
    along_z = jnp.einsum('ck,tijke->tijce', slopes, volume, precision=high)
    speeds = velocity[:, :, None, None, None, None]
    rate_sum = -(speeds[0] * along_x + speeds[1] * along_y + speeds[2] * along_z) * inv_size
    jump_diff = face_traces(volume) - outside
    lift_scale = 10.0 * inv_size
    for side_id in range(6):
        normal = velocity[side_id // 2] * (2.0 * (side_id % 2) - 1.0)
        inflow = jnp.minimum(normal, 0.0)[:, None, None, None] * lift_scale * jump_diff[:, :, :, side_id]
        places = [slice(None)] * 5
        places[1 + side_id // 2] = 4 * (side_id % 2)
        rate_sum = rate_sum.at[tuple(places)].add(inflow)
    return rate_sum.reshape(tracers, 125, elements)

def per_device(array, devices_all):
    lead_count = array.shape[0]
    moved = array.reshape(lead_count, devices_all, array.shape[1] // devices_all)
    return jnp.moveaxis(moved, 1, 0).reshape(devices_all, -1)

def reference(tracer_state, inv_size, velocity, element_count, face_kind, face_owner, face_index, face_orient, hang_owner, hang_index, hang_orient, mirror):
    devices_all = N_SLAB * N_CURVE
    tracers = tracer_state.shape[0]
    faces_total = 6 * E_DEV
    interp, project, slopes = all_tables(tracer_state.dtype)
    live = jnp.arange(E_DEV * devices_all, dtype=jnp.int32) % E_DEV < jnp.repeat(element_count, E_DEV)
    peak = jnp.max(jnp.where(live, inv_size, 0.0))
    step_size = COURANT / (peak * 16.0 * 1.5)
    rank_ids = jnp.arange(devices_all, dtype=jnp.int32)[:, None]

    def resolve(owners, indices):
        offset = rank_ids - owners
        column_set = jnp.where(offset < 0, offset + NEAR, offset + NEAR - 1)
        columns = jnp.clip(column_set * SLOTS + indices, 0, 2 * NEAR * SLOTS - 1).astype(jnp.int32)
        remote_face = mirror[owners, columns]
        local_face = jnp.where(owners == rank_ids, indices, remote_face)
        return (owners * faces_total + local_face).astype(jnp.int32)
    kinds = per_device(face_kind, devices_all)
    owners = per_device(face_owner, devices_all)
    indices = per_device(face_index, devices_all)
    turns = per_device(face_orient, devices_all)
    face_source = jnp.where(kinds == 5, 0, resolve(owners, indices)).astype(jnp.int32)
    coarse_pick = jnp.where(kinds == 5, indices, 0).astype(jnp.int32)
    hang_source = resolve(per_device(hang_owner, devices_all), per_device(hang_index, devices_all))
    hang_turns = per_device(hang_orient, devices_all)

    def outside_all(state_now):
        volume = state_now.reshape(tracers, 5, 5, 5, devices_all * E_DEV)
        traces_all = face_traces(volume).reshape(tracers * 25, 6, devices_all, E_DEV)
        sources = jnp.moveaxis(traces_all, 2, 1).reshape(tracers * 25, devices_all * faces_total)

        def one_device(inputs):
            src_now, kind_now, turn_now, hsrc_now, hturn_now, pick_now = inputs
            found = exterior_traces(sources, tracers, src_now, kind_now, turn_now, hsrc_now, hturn_now, pick_now, interp, project)
            return found.reshape(tracers, 5, 5, 6, E_DEV)
        outside = lax.map(one_device, (face_source, kinds, turns, hang_source, hang_turns, coarse_pick))
        return jnp.moveaxis(outside, 0, -2).reshape(tracers, 5, 5, 6, devices_all * E_DEV)
    first_step = step_size * tendency(tracer_state, inv_size, outside_all(tracer_state), velocity, slopes)
    middle = tracer_state + B_ONE * first_step
    second_step = A_TWO * first_step + step_size * tendency(middle, inv_size, outside_all(middle), velocity, slopes)
    finished = middle + B_TWO * second_step
    return (jnp.where(live, finished, 0.0), jnp.where(live, second_step, 0.0))
```

```python
import functools
import math

import jax
import jax.numpy as jnp
import numpy as np
from jax import lax
from jax.experimental import pallas as pl
from jax.experimental.pallas import tpu as pltpu
from jax.sharding import PartitionSpec as P

NEAR = 4
B_ONE = 1432997174477.0 / 9575080441755.0
A_TWO = -567301805773.0 / 1357537059087.0
B_TWO = 5161836677717.0 / 13612068292357.0
COURANT = 0.3
MESH = pl.DeviceIdType.MESH
OFFSETS = tuple(range(-NEAR, 0)) + tuple(range(1, NEAR + 1))
PACK = 19
ROWS = 8 * PACK
HALF = ROWS + 8


def node_tables():
    points = np.array([-1.0, -math.sqrt(3.0 / 7.0), 0.0, math.sqrt(3.0 / 7.0), 1.0])
    weights = np.array([0.1, 49.0 / 90.0, 32.0 / 45.0, 49.0 / 90.0, 0.1])
    return (points, weights)


def lagrange_at(points, targets):
    values = np.ones((len(targets), len(points)))
    for column in range(len(points)):
        for another in range(len(points)):
            if another != column:
                values[:, column] *= (targets - points[another]) / (
                    points[column] - points[another]
                )
    return values


def derivative_table(points):
    count = len(points)
    scaled = [
        np.prod([points[c] - points[o] for o in range(count) if o != c]) for c in range(count)
    ]
    result = np.zeros((count, count))
    for r in range(count):
        for c in range(count):
            if r != c:
                result[r, c] = scaled[r] / scaled[c] / (points[r] - points[c])
        result[r, r] = sum(1.0 / (points[r] - points[o]) for o in range(count) if o != r)
    result[count // 2, count // 2] = 0.0
    return result


def tables():
    points, weights = node_tables()
    interp = lagrange_at(points, (points - 1.0) / 2.0)
    project = 0.5 * (interp.T * weights[None, :]) / weights[:, None]
    return interp, project, derivative_table(points)


INTERP, PROJECT, SLOPES = tables()


def combine(row, values):
    total = None
    for factor, value in zip(row, values):
        factor = float(factor)
        if abs(factor) < 1e-14:
            continue
        term = value if factor == 1.0 else factor * value
        total = term if total is None else total + term
    return total


def flipped(grid, first, second):
    half = [
        [grid[a][b] if a == 2 else jnp.where(first, grid[4 - a][b], grid[a][b]) for b in range(5)]
        for a in range(5)
    ]
    return [
        [half[a][b] if b == 2 else jnp.where(second, half[a][4 - b], half[a][b]) for b in range(5)]
        for a in range(5)
    ]


def mapped(grid, matrix):
    along = [
        [combine(matrix[a], [grid[i][b] for i in range(5)]) for b in range(5)] for a in range(5)
    ]
    return [
        [combine(matrix[b], [along[a][j] for j in range(5)]) for b in range(5)] for a in range(5)
    ]


def split_rows(block):
    block = jnp.concatenate([block, jnp.zeros((8, block.shape[1]), jnp.float32)], axis=0)
    high = block.astype(jnp.bfloat16)
    low = (block - high.astype(jnp.float32)).astype(jnp.bfloat16)
    return jnp.concatenate([high, low], axis=0)


def picked(parts, hot):
    both = jnp.dot(parts, hot, preferred_element_type=jnp.float32)
    return both[:ROWS] + both[HALF : HALF + ROWS]


def one_hot(index_row, depth):
    places = lax.broadcasted_iota(jnp.int32, (depth, index_row.shape[1]), 0)
    return jnp.where(places == index_row, 1.0, 0.0).astype(jnp.bfloat16)


def kernel(
    sizes,
    state,
    inv,
    vel,
    count,
    kind,
    owner,
    index,
    orient,
    hang_owner,
    hang_index,
    hang_orient,
    mirror,
    new_state,
    increment,
    middle,
    first,
    rate,
    packed,
    parts,
    hot_send,
    hot_local,
    hot_far,
    pick_local,
    pick_far,
    gathered,
    outside,
    outgoing,
    incoming,
    peak_curve,
    peak_slab,
    send_sem,
    recv_sem,
    curve_send,
    curve_recv,
    slab_send,
    slab_recv,
):
    n_slab, n_curve = sizes
    n_all = n_slab * n_curve
    slab, curve = lax.axis_index("slab"), lax.axis_index("curve")
    me = slab * n_curve + curve
    elements = state.shape[4]
    faces = 6 * elements
    slots = mirror.shape[1] // len(OFFSETS)

    def at(rank):
        return (rank // n_curve, rank % n_curve)

    def inside(rank):
        return jnp.logical_and(rank >= 0, rank < n_all)

    barrier = pltpu.get_barrier_semaphore()
    greeted = jnp.int32(n_curve + n_slab - 2)
    for offset in OFFSETS:
        other = me + offset
        greeted = greeted + inside(other).astype(jnp.int32)

        @pl.when(inside(other))
        def _():
            pl.semaphore_signal(barrier, inc=1, device_id=at(other), device_id_type=MESH)

    @pl.loop(1, n_curve)
    def _(k):
        pl.semaphore_signal(
            barrier, inc=1, device_id=(slab, (curve + k) % n_curve), device_id_type=MESH
        )

    @pl.loop(1, n_slab)
    def _(k):
        pl.semaphore_signal(
            barrier, inc=1, device_id=((slab + k) % n_slab, curve), device_id_type=MESH
        )

    for c in range(len(OFFSETS) // 2):
        hot_send[c] = one_hot(mirror[:, c * 2 * slots : (c + 1) * 2 * slots], faces)

    def pack_traces(source):
        def node(s, n):
            a, b = n // 5, n % 5
            end = 4 * (s % 2)
            if s < 2:
                return source[end, a, b]
            if s < 4:
                return source[a, end, b]
            return source[a, b, end]

        low_rows = lax.broadcasted_iota(jnp.int32, (8, elements), 0) < 6
        for s in range(6):
            cols = slice(s * elements, (s + 1) * elements)
            for n in range(PACK):
                value = node(s, n)
                if n < 18:
                    extra = node(s, PACK + n // 3)
                    j = n % 3
                    moved = pltpu.roll(extra, (6 - 2 * j) % 8, 0)
                    value = jnp.where(low_rows, value, moved)
                packed[8 * n : 8 * n + 8, cols] = value
        parts[...] = split_rows(packed[...])

    def copy(round_at, c):
        return pltpu.make_async_remote_copy(
            src_ref=outgoing.at[round_at, c],
            dst_ref=incoming.at[round_at, c],
            send_sem=send_sem.at[round_at, c],
            recv_sem=recv_sem.at[round_at, c],
            device_id=at(me + OFFSETS[c]),
            device_id_type=MESH,
        )

    def send_traces(round_at):
        for pair in (0, 3, 1, 2):
            block = picked(parts[...], hot_send[pair])
            outgoing[round_at, 2 * pair] = block[:, :slots]
            outgoing[round_at, 2 * pair + 1] = block[:, slots:]
            for c in (2 * pair, 2 * pair + 1):

                @pl.when(inside(me + OFFSETS[c]))
                def _():
                    copy(round_at, c).start()

    def await_traces(round_at):
        for c in range(len(OFFSETS)):

            @pl.when(inside(me - OFFSETS[c]))
            def _():
                copy(round_at, c).wait_recv()

            @pl.when(inside(me + OFFSETS[c]))
            def _():
                copy(round_at, c).wait_send()

    def local_part():
        @pl.loop(0, 7)
        def _(j):
            gathered[j] = picked(parts[...], hot_local[j])

    def far_part(round_at):
        block = jnp.concatenate(
            [incoming[round_at, c] for c in range(len(OFFSETS))], axis=1
        )
        far = split_rows(block)

        @pl.loop(0, 7)
        def _(j):
            gathered[j] += picked(far, hot_far[j])

    def volume_rate(source):
        scale = [-(vel[d] * inv[...]) for d in range(3)]
        for a in range(5):
            rate[a] = scale[0] * combine(SLOPES[a], [source[i] for i in range(5)])
        for b in range(5):
            rate[:, b] += scale[1] * combine(SLOPES[b], [source[:, i] for i in range(5)])
        for c in range(5):
            rate[:, :, c] += scale[2] * combine(SLOPES[c], [source[:, :, i] for i in range(5)])

    def nodes_of(j, cols):
        rows = lax.broadcasted_iota(jnp.int32, (8, cols.stop - cols.start), 0)

        def group(n):
            return gathered[j, 8 * n : 8 * n + 8, cols]

        nodes = [group(n) for n in range(PACK)]
        for k in range(6):
            base = 3 * k
            nodes.append(
                jnp.where(
                    rows < 2,
                    pltpu.roll(group(base), 2, 0),
                    jnp.where(
                        rows < 4,
                        pltpu.roll(group(base + 1), 4, 0),
                        pltpu.roll(group(base + 2), 6, 0),
                    ),
                )
            )
        return [[nodes[5 * a + b] for b in range(5)] for a in range(5)]

    def coarse_faces():
        entries = hang_orient.shape[1]
        turns = jnp.concatenate([hang_orient[c : c + 1] for c in range(4)], axis=1)
        children = lax.broadcasted_iota(jnp.int32, (1, 4 * entries), 1) // entries
        totals = None
        for half in range(2):
            cols = slice(half * 2 * entries, (half + 1) * 2 * entries)
            turn, child = turns[:, cols], children[:, cols]
            grid = nodes_of(6, cols)
            grid = flipped(
                grid,
                jnp.broadcast_to(((turn ^ child) & 1) == 1, (8, 2 * entries)),
                jnp.broadcast_to(((turn ^ child) & 2) == 2, (8, 2 * entries)),
            )
            grid = mapped(grid, PROJECT)
            grid = flipped(
                grid,
                jnp.broadcast_to((child & 1) == 1, (8, 2 * entries)),
                jnp.broadcast_to((child & 2) == 2, (8, 2 * entries)),
            )
            flat = [value for line in grid for value in line]
            totals = flat if totals is None else [x + y for x, y in zip(totals, flat)]
        return [x + pltpu.roll(x, entries, 1) for x in totals]

    def face_values():
        coarse = coarse_faces()
        for n in range(25):
            outside[3, n, :, 0:128] = coarse[n]
        for d in range(3):
            for half in range(elements // 128):
                cols = slice(half * 128, (half + 1) * 128)
                positive = vel[d, :, cols] > 0.0
                even, odd = nodes_of(2 * d, cols), nodes_of(2 * d + 1, cols)
                grid = [
                    [jnp.where(positive, even[a][b], odd[a][b]) for b in range(5)]
                    for a in range(5)
                ]

                def chosen(table):
                    return jnp.where(
                        positive, table[2 * d : 2 * d + 1, cols], table[2 * d + 1 : 2 * d + 2, cols]
                    )

                kinds, turns, places = chosen(kind), chosen(orient), chosen(index)
                fine = jnp.logical_and(kinds >= 1, kinds <= 4)
                child = jnp.where(fine, kinds - 1, 0)
                grid = flipped(
                    grid, ((turns ^ child) & 1) == 1, ((turns ^ child) & 2) == 2
                )
                finer = mapped(grid, INTERP)
                grid = [
                    [jnp.where(fine, finer[a][b], grid[a][b]) for b in range(5)] for a in range(5)
                ]
                grid = flipped(grid, (child & 1) == 1, (child & 2) == 2)
                is_coarse = kinds == 5
                place = jnp.where(is_coarse, places, 0)
                for n in range(25):
                    from_children = jnp.take_along_axis(
                        outside[3, n, :, 0:128], place, axis=1
                    )
                    outside[d, n, :, cols] = jnp.where(
                        is_coarse, from_children, grid[n // 5][n % 5]
                    )

    def face_rate(source):
        for d in range(3):
            positive = vel[d] > 0.0
            scale = -(jnp.abs(vel[d]) * (10.0 * inv[...]))

            def side(ref, end):
                return (ref.at[end], ref.at[:, end], ref.at[:, :, end])[d]

            around = outside[d].reshape(5, 5, 8, elements)
            inner = jnp.where(positive, side(source, 0)[...], side(source, 4)[...])
            flow = scale * (inner - around)
            side(rate, 0)[...] += jnp.where(positive, flow, 0.0)
            side(rate, 4)[...] += jnp.where(positive, 0.0, flow)

    live = lax.broadcasted_iota(jnp.int32, (1, elements), 1) < count[0]
    peak = jnp.max(jnp.where(live, inv[...], 0.0), axis=1, keepdims=True)
    peak_curve[0] = jnp.broadcast_to(peak, (8, 128))

    def curve_copy(k):
        return pltpu.make_async_remote_copy(
            src_ref=peak_curve.at[0],
            dst_ref=peak_curve.at[k],
            send_sem=curve_send.at[k],
            recv_sem=curve_recv.at[k],
            device_id=(slab, (curve + k) % n_curve),
            device_id_type=MESH,
        )

    def slab_copy(k):
        return pltpu.make_async_remote_copy(
            src_ref=peak_slab.at[0],
            dst_ref=peak_slab.at[k],
            send_sem=slab_send.at[k],
            recv_sem=slab_recv.at[k],
            device_id=((slab + k) % n_slab, curve),
            device_id_type=MESH,
        )

    pack_traces(state)
    pl.semaphore_wait(barrier, greeted)

    @pl.loop(1, n_curve)
    def _(k):
        curve_copy(k).start()

    send_traces(0)
    for c in range(len(OFFSETS)):

        @pl.when(jnp.logical_not(inside(me - OFFSETS[c])))
        def _():
            for round_at in range(2):
                incoming[round_at, c] = jnp.zeros((ROWS, slots), jnp.float32)

    def picks(owners, indices, usable):
        here = owners == me
        offset = me - owners
        column = jnp.where(offset < 0, offset + NEAR, offset + NEAR - 1)
        near = jnp.where(jnp.logical_and(usable, here), indices, -1)
        away = jnp.logical_and(usable, jnp.logical_not(here))
        return near, jnp.where(away, column * slots + indices, -1)

    near, away = picks(owner[...], index[...], kind[...] != 5)
    for s in range(6):
        pick_local[s] = near[s : s + 1]
        pick_far[s] = away[s : s + 1]
    near, away = picks(hang_owner[...], hang_index[...], hang_index[...] >= 0)
    pick_local[6] = jnp.concatenate([near[c : c + 1] for c in range(4)], axis=1)
    pick_far[6] = jnp.concatenate([away[c : c + 1] for c in range(4)], axis=1)

    @pl.loop(0, 7)
    def _(j):
        hot_local[j] = one_hot(pick_local[j], faces)

    @pl.loop(1, n_curve)
    def _(k):
        curve_copy(k).wait()

    peak_slab[0] = jnp.max(peak_curve[...], axis=0)

    @pl.loop(1, n_slab)
    def _(k):
        slab_copy(k).start()

    local_part()

    @pl.loop(0, 7)
    def _(j):
        hot_far[j] = one_hot(pick_far[j], slots * len(OFFSETS))

    volume_rate(state)

    @pl.loop(1, n_slab)
    def _(k):
        slab_copy(k).wait()

    peak_all = jnp.max(peak_slab[...], axis=0)
    step = COURANT / (peak_all * 16.0 * 1.5)
    step = jnp.concatenate([step] * (elements // 128), axis=1)

    await_traces(0)
    far_part(0)
    face_values()
    face_rate(state)
    for a in range(5):
        now = step * rate[a]
        first[a] = now
        middle[a] = state[a] + B_ONE * now

    pack_traces(middle)
    send_traces(1)
    local_part()
    volume_rate(middle)
    await_traces(1)
    far_part(1)
    face_values()
    face_rate(middle)
    for a in range(5):
        now = A_TWO * first[a] + step * rate[a]
        increment[a] = jnp.where(live, now, 0.0)
        new_state[a] = jnp.where(live, middle[a] + B_TWO * now, 0.0)


def per_device(sizes, tracer_state, inv_size, velocity, element_count, *rest):
    tracers, _, elements = tracer_state.shape
    hanging = rest[4].shape[1]
    slots = rest[7].shape[1] // len(OFFSETS)
    faces = 6 * elements
    state = jnp.pad(jnp.swapaxes(tracer_state, 0, 1), ((0, 0), (0, 8 - tracers), (0, 0)))
    state = state.reshape(5, 5, 5, 8, elements)
    vel = jnp.broadcast_to(
        jnp.pad(velocity, ((0, 0), (0, 8 - tracers)))[:, :, None], (3, 8, elements)
    )
    vmem = pl.BlockSpec(memory_space=pltpu.VMEM)
    smem = pl.BlockSpec(memory_space=pltpu.SMEM)
    grid_shape = (5, 5, 5, 8, elements)
    f32, bf16 = jnp.float32, jnp.bfloat16
    new_state, increment = pl.pallas_call(
        functools.partial(kernel, sizes),
        out_shape=[jax.ShapeDtypeStruct(grid_shape, f32)] * 2,
        in_specs=[vmem, vmem, vmem, smem] + [vmem] * 8,
        out_specs=[vmem, vmem],
        scratch_shapes=[
            pltpu.VMEM(grid_shape, f32),
            pltpu.VMEM(grid_shape, f32),
            pltpu.VMEM(grid_shape, f32),
            pltpu.VMEM((ROWS, faces), f32),
            pltpu.VMEM((2 * HALF, faces), bf16),
            pltpu.VMEM((len(OFFSETS) // 2, faces, 2 * slots), bf16),
            pltpu.VMEM((7, faces, elements), bf16),
            pltpu.VMEM((7, len(OFFSETS) * slots, elements), bf16),
            pltpu.VMEM((7, 1, elements), jnp.int32),
            pltpu.VMEM((7, 1, elements), jnp.int32),
            pltpu.VMEM((7, ROWS, elements), f32),
            pltpu.VMEM((4, 25, 8, elements), f32),
            pltpu.VMEM((2, len(OFFSETS), ROWS, slots), f32),
            pltpu.VMEM((2, len(OFFSETS), ROWS, slots), f32),
            pltpu.VMEM((sizes[1], 8, 128), f32),
            pltpu.VMEM((sizes[0], 8, 128), f32),
            pltpu.SemaphoreType.DMA((2, len(OFFSETS))),
            pltpu.SemaphoreType.DMA((2, len(OFFSETS))),
            pltpu.SemaphoreType.DMA((sizes[1],)),
            pltpu.SemaphoreType.DMA((sizes[1],)),
            pltpu.SemaphoreType.DMA((sizes[0],)),
            pltpu.SemaphoreType.DMA((sizes[0],)),
        ],
        compiler_params=pltpu.CompilerParams(
            collective_id=0, has_side_effects=True, vmem_limit_bytes=56 * 1024 * 1024
        ),
    )(state, inv_size.reshape(1, elements), vel, element_count, *rest)

    def back(block):
        return jnp.swapaxes(block.reshape(125, 8, elements)[:, :tracers], 0, 1)

    return back(new_state), back(increment)


def solution(mesh):
    both = ("slab", "curve")
    spread = P(None, both)
    in_specs = (P(None, None, both), P(both), P(), P(both)) + (spread,) * 7 + (P(both, None),)
    out_specs = (P(None, None, both), P(None, None, both))
    return jax.shard_map(
        functools.partial(per_device, (mesh.shape["slab"], mesh.shape["curve"])),
        mesh=mesh,
        in_specs=in_specs,
        out_specs=out_specs,
        check_vma=False,
    )
```

```python
import functools
import math

import jax
import jax.numpy as jnp
import numpy as np
from jax import lax
from jax.experimental import pallas as pl
from jax.experimental.pallas import tpu as pltpu
from jax.sharding import PartitionSpec as P

NEAR = 4
B_ONE = 1432997174477.0 / 9575080441755.0
A_TWO = -567301805773.0 / 1357537059087.0
B_TWO = 5161836677717.0 / 13612068292357.0
COURANT = 0.3
MESH = pl.DeviceIdType.MESH
OFFSETS = tuple(range(-NEAR, 0)) + tuple(range(1, NEAR + 1))
PACK = 19
ROWS = 8 * PACK
HALF = ROWS + 8


def node_tables():
    points = np.array([-1.0, -math.sqrt(3.0 / 7.0), 0.0, math.sqrt(3.0 / 7.0), 1.0])
    weights = np.array([0.1, 49.0 / 90.0, 32.0 / 45.0, 49.0 / 90.0, 0.1])
    return (points, weights)


def lagrange_at(points, targets):
    values = np.ones((len(targets), len(points)))
    for column in range(len(points)):
        for another in range(len(points)):
            if another != column:
                values[:, column] *= (targets - points[another]) / (
                    points[column] - points[another]
                )
    return values


def derivative_table(points):
    count = len(points)
    scaled = [
        np.prod([points[c] - points[o] for o in range(count) if o != c]) for c in range(count)
    ]
    result = np.zeros((count, count))
    for r in range(count):
        for c in range(count):
            if r != c:
                result[r, c] = scaled[r] / scaled[c] / (points[r] - points[c])
        result[r, r] = sum(1.0 / (points[r] - points[o]) for o in range(count) if o != r)
    result[count // 2, count // 2] = 0.0
    return result


def tables():
    points, weights = node_tables()
    interp = lagrange_at(points, (points - 1.0) / 2.0)
    project = 0.5 * (interp.T * weights[None, :]) / weights[:, None]
    return interp, project, derivative_table(points)


INTERP, PROJECT, SLOPES = tables()


def combine(row, values):
    total = None
    for factor, value in zip(row, values):
        factor = float(factor)
        if abs(factor) < 1e-14:
            continue
        term = value if factor == 1.0 else factor * value
        total = term if total is None else total + term
    return total


def flipped(grid, first, second):
    half = [
        [grid[a][b] if a == 2 else jnp.where(first, grid[4 - a][b], grid[a][b]) for b in range(5)]
        for a in range(5)
    ]
    return [
        [half[a][b] if b == 2 else jnp.where(second, half[a][4 - b], half[a][b]) for b in range(5)]
        for a in range(5)
    ]


def mapped(grid, matrix):
    along = [
        [combine(matrix[a], [grid[i][b] for i in range(5)]) for b in range(5)] for a in range(5)
    ]
    return [
        [combine(matrix[b], [along[a][j] for j in range(5)]) for b in range(5)] for a in range(5)
    ]


def split_rows(block):
    block = jnp.concatenate([block, jnp.zeros((8, block.shape[1]), jnp.float32)], axis=0)
    high = block.astype(jnp.bfloat16)
    low = (block - high.astype(jnp.float32)).astype(jnp.bfloat16)
    return jnp.concatenate([high, low], axis=0)


def picked(parts, hot):
    both = jnp.dot(parts, hot, preferred_element_type=jnp.float32)
    return both[:ROWS] + both[HALF : HALF + ROWS]


def one_hot(index_row, depth):
    places = lax.broadcasted_iota(jnp.int32, (depth, index_row.shape[1]), 0)
    return jnp.where(places == index_row, 1.0, 0.0).astype(jnp.bfloat16)


def kernel(
    sizes,
    state,
    inv,
    speeds,
    count,
    kind,
    owner,
    index,
    orient,
    hang_owner,
    hang_index,
    hang_orient,
    mirror,
    new_state,
    increment,
    middle,
    first,
    rate,
    packed,
    parts,
    hot_send,
    hot_local,
    hot_far,
    pick_local,
    pick_far,
    gathered,
    outside,
    vel,
    outgoing,
    incoming,
    peak_curve,
    peak_slab,
    send_sem,
    recv_sem,
    curve_send,
    curve_recv,
    slab_send,
    slab_recv,
):
    n_slab, n_curve = sizes
    n_all = n_slab * n_curve
    slab, curve = lax.axis_index("slab"), lax.axis_index("curve")
    me = slab * n_curve + curve
    elements = state.shape[4]
    faces = 6 * elements
    slots = mirror.shape[1] // len(OFFSETS)

    def at(rank):
        return (rank // n_curve, rank % n_curve)

    def inside(rank):
        return jnp.logical_and(rank >= 0, rank < n_all)

    barrier = pltpu.get_barrier_semaphore()
    greeted = jnp.int32(n_curve + n_slab - 2)
    for offset in OFFSETS:
        other = me + offset
        greeted = greeted + inside(other).astype(jnp.int32)

        @pl.when(inside(other))
        def _():
            pl.semaphore_signal(barrier, inc=1, device_id=at(other), device_id_type=MESH)

    @pl.loop(1, n_curve)
    def _(k):
        pl.semaphore_signal(
            barrier, inc=1, device_id=(slab, (curve + k) % n_curve), device_id_type=MESH
        )

    @pl.loop(1, n_slab)
    def _(k):
        pl.semaphore_signal(
            barrier, inc=1, device_id=((slab + k) % n_slab, curve), device_id_type=MESH
        )

    tracer_row = lax.broadcasted_iota(jnp.int32, (8, elements), 0)
    for d in range(3):
        line = jnp.zeros((8, elements), jnp.float32)
        for t in range(speeds.shape[1]):
            line = jnp.where(tracer_row == t, speeds[d, t], line)
        vel[d] = line

    for c in range(len(OFFSETS) // 2):
        hot_send[c] = one_hot(mirror[:, c * 2 * slots : (c + 1) * 2 * slots], faces)

    def pack_traces(source):
        def node(s, n):
            a, b = n // 5, n % 5
            end = 4 * (s % 2)
            if s < 2:
                return source[end, a, b]
            if s < 4:
                return source[a, end, b]
            return source[a, b, end]

        low_rows = lax.broadcasted_iota(jnp.int32, (8, elements), 0) < 6
        for s in range(6):
            cols = slice(s * elements, (s + 1) * elements)
            for n in range(PACK):
                value = node(s, n)
                if n < 18:
                    extra = node(s, PACK + n // 3)
                    j = n % 3
                    moved = pltpu.roll(extra, (6 - 2 * j) % 8, 0)
                    value = jnp.where(low_rows, value, moved)
                packed[8 * n : 8 * n + 8, cols] = value
        parts[...] = split_rows(packed[...])

    def copy(round_at, c):
        return pltpu.make_async_remote_copy(
            src_ref=outgoing.at[round_at, c],
            dst_ref=incoming.at[round_at, c],
            send_sem=send_sem.at[round_at, c],
            recv_sem=recv_sem.at[round_at, c],
            device_id=at(me + OFFSETS[c]),
            device_id_type=MESH,
        )

    def send_traces(round_at):
        for pair in (0, 3, 1, 2):
            block = picked(parts[...], hot_send[pair])
            outgoing[round_at, 2 * pair] = block[:, :slots]
            outgoing[round_at, 2 * pair + 1] = block[:, slots:]
            for c in (2 * pair, 2 * pair + 1):

                @pl.when(inside(me + OFFSETS[c]))
                def _():
                    copy(round_at, c).start()

    def await_sent(round_at):
        for c in range(len(OFFSETS)):

            @pl.when(inside(me + OFFSETS[c]))
            def _():
                copy(round_at, c).wait_send()

    def local_part():
        @pl.loop(0, 7)
        def _(j):
            gathered[j] = picked(parts[...], hot_local[j])

    def far_part(round_at):
        for pair in (1, 2, 0, 3):
            for c in (2 * pair, 2 * pair + 1):

                @pl.when(inside(me - OFFSETS[c]))
                def _():
                    copy(round_at, c).wait_recv()

            far = split_rows(
                jnp.concatenate(
                    [incoming[round_at, 2 * pair], incoming[round_at, 2 * pair + 1]], axis=1
                )
            )

            @pl.loop(0, 7)
            def _(j):
                rows = slice(2 * pair * slots, 2 * (pair + 1) * slots)
                gathered[j] += picked(far, hot_far[j, rows, :])

    def volume_rate(source):
        scale = [-(vel[d] * inv[...]) for d in range(3)]
        for a in range(5):
            rate[a] = scale[0] * combine(SLOPES[a], [source[i] for i in range(5)])
        for b in range(5):
            rate[:, b] += scale[1] * combine(SLOPES[b], [source[:, i] for i in range(5)])
        for c in range(5):
            rate[:, :, c] += scale[2] * combine(SLOPES[c], [source[:, :, i] for i in range(5)])

    def nodes_of(j, cols):
        rows = lax.broadcasted_iota(jnp.int32, (8, cols.stop - cols.start), 0)

        def group(n):
            return gathered[j, 8 * n : 8 * n + 8, cols]

        nodes = [group(n) for n in range(PACK)]
        for k in range(6):
            base = 3 * k
            nodes.append(
                jnp.where(
                    rows < 2,
                    pltpu.roll(group(base), 2, 0),
                    jnp.where(
                        rows < 4,
                        pltpu.roll(group(base + 1), 4, 0),
                        pltpu.roll(group(base + 2), 6, 0),
                    ),
                )
            )
        return [[nodes[5 * a + b] for b in range(5)] for a in range(5)]

    def coarse_faces():
        entries = hang_orient.shape[1]
        turns = jnp.concatenate([hang_orient[c : c + 1] for c in range(4)], axis=1)
        children = lax.broadcasted_iota(jnp.int32, (1, 4 * entries), 1) // entries
        totals = None
        for half in range(2):
            cols = slice(half * 2 * entries, (half + 1) * 2 * entries)
            turn, child = turns[:, cols], children[:, cols]
            grid = nodes_of(6, cols)
            grid = flipped(
                grid,
                jnp.broadcast_to(((turn ^ child) & 1) == 1, (8, 2 * entries)),
                jnp.broadcast_to(((turn ^ child) & 2) == 2, (8, 2 * entries)),
            )
            grid = mapped(grid, PROJECT)
            grid = flipped(
                grid,
                jnp.broadcast_to((child & 1) == 1, (8, 2 * entries)),
                jnp.broadcast_to((child & 2) == 2, (8, 2 * entries)),
            )
            flat = [value for line in grid for value in line]
            totals = flat if totals is None else [x + y for x, y in zip(totals, flat)]
        return [x + pltpu.roll(x, entries, 1) for x in totals]

    def face_values():
        coarse = coarse_faces()
        for n in range(25):
            outside[3, n, :, 0:128] = coarse[n]
        for d in range(3):
            for half in range(elements // 128):
                cols = slice(half * 128, (half + 1) * 128)
                positive = vel[d, :, cols] > 0.0
                even, odd = nodes_of(2 * d, cols), nodes_of(2 * d + 1, cols)
                grid = [
                    [jnp.where(positive, even[a][b], odd[a][b]) for b in range(5)]
                    for a in range(5)
                ]

                def chosen(table):
                    return jnp.where(
                        positive, table[2 * d : 2 * d + 1, cols], table[2 * d + 1 : 2 * d + 2, cols]
                    )

                kinds, turns, places = chosen(kind), chosen(orient), chosen(index)
                fine = jnp.logical_and(kinds >= 1, kinds <= 4)
                child = jnp.where(fine, kinds - 1, 0)
                grid = flipped(
                    grid, ((turns ^ child) & 1) == 1, ((turns ^ child) & 2) == 2
                )
                finer = mapped(grid, INTERP)
                grid = [
                    [jnp.where(fine, finer[a][b], grid[a][b]) for b in range(5)] for a in range(5)
                ]
                grid = flipped(grid, (child & 1) == 1, (child & 2) == 2)
                is_coarse = kinds == 5
                place = jnp.where(is_coarse, places, 0)
                for n in range(25):
                    from_children = jnp.take_along_axis(
                        outside[3, n, :, 0:128], place, axis=1
                    )
                    outside[d, n, :, cols] = jnp.where(
                        is_coarse, from_children, grid[n // 5][n % 5]
                    )

    def face_rate(source):
        for d in range(3):
            positive = vel[d] > 0.0
            scale = -(jnp.abs(vel[d]) * (10.0 * inv[...]))

            def side(ref, end):
                return (ref.at[end], ref.at[:, end], ref.at[:, :, end])[d]

            around = outside[d].reshape(5, 5, 8, elements)
            inner = jnp.where(positive, side(source, 0)[...], side(source, 4)[...])
            flow = scale * (inner - around)
            side(rate, 0)[...] += jnp.where(positive, flow, 0.0)
            side(rate, 4)[...] += jnp.where(positive, 0.0, flow)

    live = lax.broadcasted_iota(jnp.int32, (1, elements), 1) < count[0]
    peak = jnp.max(jnp.where(live, inv[...], 0.0), axis=1, keepdims=True)
    peak_curve[0] = jnp.broadcast_to(peak, (8, 128))

    def curve_copy(k):
        return pltpu.make_async_remote_copy(
            src_ref=peak_curve.at[0],
            dst_ref=peak_curve.at[k],
            send_sem=curve_send.at[k],
            recv_sem=curve_recv.at[k],
            device_id=(slab, (curve + k) % n_curve),
            device_id_type=MESH,
        )

    def slab_copy(k):
        return pltpu.make_async_remote_copy(
            src_ref=peak_slab.at[0],
            dst_ref=peak_slab.at[k],
            send_sem=slab_send.at[k],
            recv_sem=slab_recv.at[k],
            device_id=((slab + k) % n_slab, curve),
            device_id_type=MESH,
        )

    pack_traces(state)
    pl.semaphore_wait(barrier, greeted)

    @pl.loop(1, n_curve)
    def _(k):
        curve_copy(k).start()

    send_traces(0)
    for c in range(len(OFFSETS)):

        @pl.when(jnp.logical_not(inside(me - OFFSETS[c])))
        def _():
            for round_at in range(2):
                incoming[round_at, c] = jnp.zeros((ROWS, slots), jnp.float32)

    def picks(owners, indices, usable):
        here = owners == me
        offset = me - owners
        column = jnp.where(offset < 0, offset + NEAR, offset + NEAR - 1)
        near = jnp.where(jnp.logical_and(usable, here), indices, -1)
        away = jnp.logical_and(usable, jnp.logical_not(here))
        return near, jnp.where(away, column * slots + indices, -1)

    near, away = picks(owner[...], index[...], kind[...] != 5)
    for s in range(6):
        pick_local[s] = near[s : s + 1]
        pick_far[s] = away[s : s + 1]
    near, away = picks(hang_owner[...], hang_index[...], hang_index[...] >= 0)
    pick_local[6] = jnp.concatenate([near[c : c + 1] for c in range(4)], axis=1)
    pick_far[6] = jnp.concatenate([away[c : c + 1] for c in range(4)], axis=1)

    @pl.loop(0, 7)
    def _(j):
        hot_local[j] = one_hot(pick_local[j], faces)

    @pl.loop(1, n_curve)
    def _(k):
        curve_copy(k).wait()

    peak_slab[0] = jnp.max(peak_curve[...], axis=0)

    @pl.loop(1, n_slab)
    def _(k):
        slab_copy(k).start()

    local_part()

    @pl.loop(0, 7)
    def _(j):
        hot_far[j] = one_hot(pick_far[j], slots * len(OFFSETS))

    volume_rate(state)

    @pl.loop(1, n_slab)
    def _(k):
        slab_copy(k).wait()

    peak_all = jnp.max(peak_slab[...], axis=0)
    step = COURANT / (peak_all * 16.0 * 1.5)
    step = jnp.concatenate([step] * (elements // 128), axis=1)

    far_part(0)
    face_values()
    face_rate(state)
    for a in range(5):
        now = step * rate[a]
        first[a] = now
        middle[a] = state[a] + B_ONE * now

    pack_traces(middle)
    send_traces(1)
    local_part()
    volume_rate(middle)
    far_part(1)
    face_values()
    face_rate(middle)
    for a in range(5):
        now = A_TWO * first[a] + step * rate[a]
        increment[a] = jnp.where(live, now, 0.0)
        new_state[a] = jnp.where(live, middle[a] + B_TWO * now, 0.0)
    await_sent(0)
    await_sent(1)


def per_device(sizes, tracer_state, inv_size, velocity, element_count, *rest):
    tracers, _, elements = tracer_state.shape
    hanging = rest[4].shape[1]
    slots = rest[7].shape[1] // len(OFFSETS)
    faces = 6 * elements
    state = jnp.pad(jnp.swapaxes(tracer_state, 0, 1), ((0, 0), (0, 8 - tracers), (0, 0)))
    state = state.reshape(5, 5, 5, 8, elements)
    vmem = pl.BlockSpec(memory_space=pltpu.VMEM)
    smem = pl.BlockSpec(memory_space=pltpu.SMEM)
    grid_shape = (5, 5, 5, 8, elements)
    f32, bf16 = jnp.float32, jnp.bfloat16
    new_state, increment = pl.pallas_call(
        functools.partial(kernel, sizes),
        out_shape=[jax.ShapeDtypeStruct(grid_shape, f32)] * 2,
        in_specs=[vmem, vmem, smem, smem] + [vmem] * 8,
        out_specs=[vmem, vmem],
        scratch_shapes=[
            pltpu.VMEM(grid_shape, f32),
            pltpu.VMEM(grid_shape, f32),
            pltpu.VMEM(grid_shape, f32),
            pltpu.VMEM((ROWS, faces), f32),
            pltpu.VMEM((2 * HALF, faces), bf16),
            pltpu.VMEM((len(OFFSETS) // 2, faces, 2 * slots), bf16),
            pltpu.VMEM((7, faces, elements), bf16),
            pltpu.VMEM((7, len(OFFSETS) * slots, elements), bf16),
            pltpu.VMEM((7, 1, elements), jnp.int32),
            pltpu.VMEM((7, 1, elements), jnp.int32),
            pltpu.VMEM((7, ROWS, elements), f32),
            pltpu.VMEM((4, 25, 8, elements), f32),
            pltpu.VMEM((3, 8, elements), f32),
            pltpu.VMEM((2, len(OFFSETS), ROWS, slots), f32),
            pltpu.VMEM((2, len(OFFSETS), ROWS, slots), f32),
            pltpu.VMEM((sizes[1], 8, 128), f32),
            pltpu.VMEM((sizes[0], 8, 128), f32),
            pltpu.SemaphoreType.DMA((2, len(OFFSETS))),
            pltpu.SemaphoreType.DMA((2, len(OFFSETS))),
            pltpu.SemaphoreType.DMA((sizes[1],)),
            pltpu.SemaphoreType.DMA((sizes[1],)),
            pltpu.SemaphoreType.DMA((sizes[0],)),
            pltpu.SemaphoreType.DMA((sizes[0],)),
        ],
        compiler_params=pltpu.CompilerParams(
            collective_id=0, has_side_effects=True, vmem_limit_bytes=56 * 1024 * 1024
        ),
    )(state, inv_size.reshape(1, elements), velocity, element_count, *rest)

    def back(block):
        return jnp.swapaxes(block.reshape(125, 8, elements)[:, :tracers], 0, 1)

    return back(new_state), back(increment)


def solution(mesh):
    both = ("slab", "curve")
    spread = P(None, both)
    in_specs = (P(None, None, both), P(both), P(), P(both)) + (spread,) * 7 + (P(both, None),)
    out_specs = (P(None, None, both), P(None, None, both))
    return jax.shard_map(
        functools.partial(per_device, (mesh.shape["slab"], mesh.shape["curve"])),
        mesh=mesh,
        in_specs=in_specs,
        out_specs=out_specs,
        check_vma=False,
    )
```
